32 devices in a mesh: seq: 8 (over z, y), nb: 4 (over x, core).
Axes of the slice: x: 2, y: 2, z: 4, core: 2. Of those that a mesh axis runs over, the one named last changes fastest.
Arguments:
- q_self: bfloat16 [2048, 4096], P('seq', 'nb'), may hold values from -6 to 6
- k_self: bfloat16 [2048, 4096], P('seq', 'nb'), may hold values from -6 to 6
- v_self: bfloat16 [2048, 4096], P('seq', 'nb'), may hold values from -6 to 6
- q_cca: bfloat16 [2048, 4096], P('seq', 'nb'), may hold values from -6 to 6
- memory: bfloat16 [2048, 2, 1024], P('seq'), may hold values from -6 to 6
- database: bfloat16 [8192, 2048], P(('seq', 'nb')), may hold values from -6 to 6
- nbr_block: int32 [512], P(('seq', 'nb')), may hold values from 0 to 63, as said below
- span_offset: int32 [32], P('seq'), may hold values from 1 to 63
- enc_query: bfloat16 [2048, 1024], P('seq'), may hold values from -0.1355122 to 0.1355122
- enc_out: bfloat16 [1024, 2048], P('seq'), may hold values from -0.1875 to 0.1875
- enc_gain: float32 [2048], replicated, may hold values from 0.5 to 1.5
- cca_kv: bfloat16 [2048, 2, 4096], P(None, None, 'nb'), may hold values from -0.134535646 to 0.134535646
Outputs:
- attended: bfloat16 [2048, 4096], P('seq', 'nb')
The draws below stay inside these ranges and needn't reach their ends.
Inputs may be any that keep to these rules, and one draw needn't show every extreme that they name: `nbr_block`: block ids are local to a group of 4 devices along nb; the owner of id g is nb index g // 16. Among the 16 requests of one device at most 12 name blocks of one owner, and exactly 12 name blocks of some owner.
All inputs are finite; a program needn't handle non-finite values.
Results may differ from the reference program's by a relative error of at most 0.0041.
Values may be sent and summed in bfloat16 or wider, within the bound.
A program may use at most 192 MiB of HBM per device.

```python
import jax
import jax.numpy as jnp
from jax import lax

HD = 128
HEADS = 32
E = 2048
EH = 8
SPAN = 64
K = 2
R = 128
BLK = 16
DB_DEV = 16
TOKENS = 2048
SPANS = 32
REQ_DEV = 16
REQUESTS = 512
CAP = 12
DB_ROWS = 8192
N_NB = 4


def base_field(key, shape):
    return jnp.clip(jax.random.normal(key, shape, jnp.float32), -6.0, 6.0)


def sign_table(key, tag, shape):
    bits = jax.random.randint(jax.random.fold_in(key, tag), shape, 0, 2)
    return (2 * bits - 1).astype(jnp.float32)


def planted_queries(key, tag, strength_lo, strength_hi):
    signs = sign_table(key, tag, (HEADS, HD))
    rows = jnp.arange(TOKENS, dtype=jnp.int32)
    chosen = jax.random.randint(jax.random.fold_in(key, tag + 1), (TOKENS,), 0, 64) == 0
    chosen = chosen & (rows >= 8) | (rows == TOKENS - 1)
    head_pick = jax.random.randint(jax.random.fold_in(key, tag + 2), (TOKENS,), 0, HEADS)
    strength = jax.random.uniform(jax.random.fold_in(key, tag + 3), (TOKENS,), jnp.float32, strength_lo, strength_hi)
    strength = jnp.where(rows == TOKENS - 1, strength_hi, strength)
    head_hit = (head_pick[:, None] == jnp.arange(HEADS, dtype=jnp.int32)[None, :]) & chosen[:, None]
    planted = strength[:, None, None] * signs[None, :, :]
    return (head_hit, planted)


def draw_q_self(key, part):
    base = base_field(jax.random.fold_in(key, 1), (TOKENS, HEADS, HD))
    head_hit, planted = planted_queries(key, 201, 2.4, 5.4)
    return jnp.where(head_hit[:, :, None], planted, base).reshape(TOKENS, HEADS * HD).astype(jnp.bfloat16)


def draw_k_self(key, part):
    base = base_field(jax.random.fold_in(key, 2), (TOKENS, HEADS, HD))
    signs = sign_table(key, 201, (HEADS, HD))
    first = jax.random.randint(jax.random.fold_in(key, 211), (), 0, 8)
    second = (first + 1 + jax.random.randint(jax.random.fold_in(key, 212), (), 0, 7)) % 8
    rows = jnp.arange(TOKENS, dtype=jnp.int32)[:, None, None]
    field = jnp.where(rows == second, 3.953125 * signs[None], base)
    field = jnp.where(rows == first, 4.0 * signs[None], field)
    return field.reshape(TOKENS, HEADS * HD).astype(jnp.bfloat16)


def draw_q_cca(key, part):
    base = base_field(jax.random.fold_in(key, 3), (TOKENS, HEADS, HD))
    head_hit, planted = planted_queries(key, 301, 2.4, 5.5)
    return jnp.where(head_hit[:, :, None], planted, base).reshape(TOKENS, HEADS * HD).astype(jnp.bfloat16)


def draw_memory(key, part):
    base = base_field(jax.random.fold_in(key, 4), (TOKENS, 2, EH, HD))
    signs = sign_table(key, 402, (EH, HD))
    span_count = TOKENS // SPAN
    level = 2.0 + jax.random.randint(jax.random.fold_in(key, 403), (span_count,), 0, 128).astype(jnp.float32) / 64.0
    level = jnp.where(jnp.arange(span_count, dtype=jnp.int32) == 0, 3.984375, level)
    second = 1 + jax.random.randint(jax.random.fold_in(key, 404), (span_count,), 0, min(7, SPAN - 1))
    rows = jnp.arange(TOKENS, dtype=jnp.int32)
    within = rows % SPAN
    row_level = jnp.repeat(level, SPAN)
    row_second = jnp.repeat(second, SPAN)
    key_level = jnp.where(within == 0, row_level, row_level - 0.03125)
    planted = (within == 0) | (within == row_second)
    keys = jnp.where(planted[:, None, None], key_level[:, None, None] * signs[None], base[:, 0])
    return jnp.stack([keys, base[:, 1]], axis=1).reshape(TOKENS, 2, EH * HD).astype(jnp.bfloat16)


def draw_database(key, part):
    base = base_field(jax.random.fold_in(key, 5), (DB_ROWS, E))
    direction = sign_table(key, 401, (E,))
    pick = jax.random.randint(jax.random.fold_in(key, 405), (DB_ROWS // BLK,), 0, BLK)
    rows = jnp.arange(DB_ROWS, dtype=jnp.int32)
    planted = rows % BLK == jnp.repeat(pick, BLK)
    return jnp.where(planted[:, None], direction[None, :] + 0.3 * base, base).astype(jnp.bfloat16)


def draw_enc_query(key, part):
    base = base_field(jax.random.fold_in(key, 6), (E, EH * HD)) * E ** (-0.5)
    direction = sign_table(key, 401, (E,))
    head_signs = sign_table(key, 402, (EH, HD)).reshape(EH * HD)
    return (base + 6.0 / E * direction[:, None] * head_signs[None, :]).astype(jnp.bfloat16)


def draw_cca_kv(key, part):
    base = base_field(jax.random.fold_in(key, 7), (E, 2, HEADS * HD)) * E ** (-0.5)
    direction = sign_table(key, 401, (E,))
    head_signs = sign_table(key, 301, (HEADS, HD)).reshape(HEADS * HD)
    keys = base[:, 0] + 4.0 / E * direction[:, None] * head_signs[None, :]
    return jnp.stack([keys, base[:, 1]], axis=1).astype(jnp.bfloat16)


def draw_nbr_block(key, part):
    device_count = REQUESTS // REQ_DEV
    key_first = jax.random.fold_in(key, 11)
    key_second = jax.random.fold_in(key, 12)
    key_rotation = jax.random.fold_in(key, 13)
    key_order = jax.random.fold_in(key, 14)
    key_blocks = jax.random.fold_in(key, 15)
    key_labels = jax.random.fold_in(key, 16)
    hot_raw = jnp.minimum(jax.random.randint(key_first, (device_count,), 0, N_NB), jax.random.randint(key_second, (device_count,), 0, N_NB))
    relabel = jax.random.permutation(key_labels, N_NB).astype(jnp.int32)
    hot_owner = relabel[hot_raw]
    rotation = jax.random.randint(key_rotation, (device_count, 1), 0, N_NB - 1)
    column = jnp.arange(REQ_DEV, dtype=jnp.int32)[None, :]
    other_owner = (hot_owner[:, None] + 1 + (column - CAP + rotation) % (N_NB - 1)) % N_NB
    owner_ids = jnp.where(column < CAP, hot_owner[:, None], other_owner)
    order_keys = jax.random.randint(key_order, (device_count, REQ_DEV), 0, 2 ** 20) * REQ_DEV + column
    order = jnp.argsort(order_keys, axis=1, stable=True)
    owner_ids = jnp.take_along_axis(owner_ids, order, axis=1)
    block_local = jax.random.randint(key_blocks, (device_count, REQ_DEV), 0, DB_DEV)
    return (owner_ids * DB_DEV + block_local).reshape(-1).astype(jnp.int32)


def touch_ends(entries, rng, smallest, high):
    spot = [jax.random.randint(jax.random.fold_in(rng, axis), (), 0, length) for axis, length in enumerate(entries.shape)]
    main_axis = entries.shape.index(max(entries.shape))
    neighbour = spot[:main_axis] + [(spot[main_axis] + 1) % entries.shape[main_axis]] + spot[main_axis + 1:]
    return entries.at[tuple(spot)].set(smallest).at[tuple(neighbour)].set(high)


def level_of(rng, extent, pieces, least, top_value):
    factor_of = 1.0
    for dim, shards_of in pieces:
        draws = jax.random.uniform(jax.random.fold_in(jax.random.fold_in(rng, 6), dim), (shards_of,), jnp.float32, least / len(pieces), top_value / len(pieces))
        factor_of = factor_of * jnp.repeat(jnp.exp(draws), extent[dim] // shards_of).reshape((-1,) + (1,) * (len(extent) - 1 - dim))
    return factor_of


def scatter_about(rng, dims, scale, bound, pieces=(), kind=jnp.bfloat16):
    factor_of = level_of(rng, dims, pieces, -0.22, 0.18) if pieces else 1.0
    values = jax.random.normal(rng, dims, jnp.float32) * scale * factor_of
    return jnp.minimum(jnp.maximum(values, -bound), bound).astype(kind)


def setup_inputs(seed: int = 0) -> dict:
    arg_keys = jax.random.split(jax.random.key(seed), 13)
    return {
        "q_self": draw_q_self(jax.random.fold_in(arg_keys[12], 71), 0),
        "k_self": draw_k_self(jax.random.fold_in(arg_keys[12], 71), 0),
        "v_self": scatter_about(arg_keys[2], (TOKENS, HEADS * HD), 1.0, 6.0, ((0, 8), (1, 4))),
        "q_cca": draw_q_cca(jax.random.fold_in(arg_keys[12], 71), 0),
        "memory": draw_memory(jax.random.fold_in(arg_keys[12], 71), 0),
        "database": draw_database(jax.random.fold_in(arg_keys[12], 71), 0),
        "nbr_block": draw_nbr_block(jax.random.fold_in(arg_keys[12], 71), 0),
        "span_offset": touch_ends(jax.random.randint(arg_keys[7], (SPANS,), 1, SPAN), jax.random.fold_in(arg_keys[7], 1), 1, SPAN - 1).astype(jnp.int32),
        "enc_query": draw_enc_query(jax.random.fold_in(arg_keys[12], 71), 0),
        "enc_out": scatter_about(arg_keys[9], (EH * HD, E), (EH * HD) ** -0.5, 0.1875, ((0, 8),)),
        "enc_gain": jnp.clip(1.0 + 0.1 * jax.random.normal(arg_keys[10], (E,), jnp.float32), 0.5, 1.5),
        "cca_kv": draw_cca_kv(jax.random.fold_in(arg_keys[12], 71), 0),
    }


masked_score = -1e+30

def reference(q_self, k_self, v_self, q_cca, memory, database, nbr_block, span_offset, enc_query, enc_out, enc_gain, cca_kv):
    score_scale = HD ** (-0.5)
    positions = jnp.arange(TOKENS, dtype=jnp.int32)
    causal = positions[:, None] >= positions[None, :]

    def self_head(operands):
        query_h, key_h, value_h = operands
        scores = jnp.dot(query_h, key_h.T, preferred_element_type=jnp.float32) * score_scale
        scores = jnp.where(causal, scores, masked_score)
        row_max = lax.optimization_barrier(jnp.max(scores, axis=1, keepdims=True))
        weights = jnp.where(causal, jnp.exp(scores - row_max), 0.0)
        totals = lax.optimization_barrier(jnp.sum(weights, axis=1, keepdims=True))
        summed = jnp.dot(weights.astype(jnp.bfloat16), value_h, preferred_element_type=jnp.float32)
        return summed / totals

    def split_heads(array):
        return array.reshape(TOKENS, HEADS, HD).transpose(1, 0, 2)
    self_out = lax.map(self_head, (split_heads(q_self), split_heads(k_self), split_heads(v_self)))
    self_out = self_out.transpose(1, 0, 2).reshape(TOKENS, HEADS * HD)
    request_ids = jnp.arange(REQUESTS, dtype=jnp.int32)
    group_ids = request_ids // (N_NB * REQ_DEV)
    block_ids = (group_ids * (N_NB * DB_DEV) + nbr_block).astype(jnp.int32)
    nbr_rows = database.reshape(-1, BLK, E)[block_ids].reshape(SPANS, K * R, E)
    memory_spans = memory.reshape(SPANS, SPAN, 2, EH * HD)
    gain_row = enc_gain.astype(jnp.float32)

    def encode_span(operands):
        rows_in, memory_c, offset_c = operands
        wide = rows_in.astype(jnp.float32)
        normed = wide * lax.rsqrt(lax.optimization_barrier(jnp.mean(wide * wide, axis=1, keepdims=True)) + 1e-06) * gain_row
        enc_q = (jnp.dot(normed.astype(jnp.bfloat16), enc_query, preferred_element_type=jnp.float32) * score_scale).astype(jnp.bfloat16)
        enc_q = enc_q.reshape(K * R, EH, HD).astype(jnp.float32)
        key_rows = memory_c[:, 0].reshape(SPAN, EH, HD).astype(jnp.float32)
        value_rows = memory_c[:, 1].reshape(SPAN, EH, HD).astype(jnp.float32)
        scores = jnp.einsum('nhd,khd->hnk', enc_q, key_rows)
        allowed = (jnp.arange(SPAN, dtype=jnp.int32) < offset_c)[None, None, :]
        scores = jnp.where(allowed, scores, masked_score)
        row_max = lax.optimization_barrier(jnp.max(scores, axis=2, keepdims=True))
        weights = jnp.where(allowed, jnp.exp(scores - row_max), 0.0)
        totals = lax.optimization_barrier(jnp.sum(weights, axis=2))
        context = jnp.einsum('hnk,khd->nhd', weights.astype(jnp.bfloat16).astype(jnp.float32), value_rows)
        context = (context / totals.T[:, :, None]).astype(jnp.bfloat16).reshape(K * R, EH * HD)
        return (wide + jnp.dot(context, enc_out, preferred_element_type=jnp.float32)).astype(jnp.bfloat16)
    encoded = lax.map(encode_span, (nbr_rows, memory_spans, span_offset))
    weight_kv = cca_kv.reshape(E, 2 * HEADS * HD)

    def project_span(rows_in):
        return jnp.dot(rows_in, weight_kv, preferred_element_type=jnp.float32).astype(jnp.bfloat16)
    span_kv = lax.map(project_span, encoded).reshape(SPANS, K * R, 2, HEADS, HD)
    earlier_kv = jnp.concatenate([jnp.zeros_like(span_kv[:1]), span_kv[:-1]], axis=0)
    cross_queries = q_cca.reshape(SPANS, SPAN, HEADS, HD).astype(jnp.float32)

    def cross_span(operands):
        query_c, own_kv, prior_kv, offset_c = operands

        def attend_set(kv_set):
            key_rows = kv_set[:, 0].astype(jnp.float32)
            value_rows = kv_set[:, 1].astype(jnp.float32)
            scores = jnp.einsum('chd,khd->hck', query_c, key_rows) * score_scale
            row_max = lax.optimization_barrier(jnp.max(scores, axis=2, keepdims=True))
            weights = jnp.exp(scores - row_max)
            totals = lax.optimization_barrier(jnp.sum(weights, axis=2))
            summed = jnp.einsum('hck,khd->chd', weights.astype(jnp.bfloat16).astype(jnp.float32), value_rows)
            return summed / totals.T[:, :, None]
        see_own = (jnp.arange(SPAN, dtype=jnp.int32) >= offset_c)[:, None, None]
        return jnp.where(see_own, attend_set(own_kv), attend_set(prior_kv))
    cca_out = lax.map(cross_span, (cross_queries, span_kv, earlier_kv, span_offset))
    cca_out = cca_out.reshape(TOKENS, HEADS * HD)
    return (self_out + cca_out).astype(jnp.bfloat16)
```

```python
import functools

import jax
import jax.numpy as jnp
from jax import lax
from jax.experimental import pallas as pl
from jax.experimental.pallas import tpu as pltpu
from jax.sharding import PartitionSpec as P

HD = 128
SPAN = 64
K = 2
R = 128
BLK = 16
SET = K * R

masked_score = -1e30
MESH = pl.DeviceIdType.MESH
DOT_T = (((1,), (1,)), ((), ()))
LIMIT = 56 * 1024 * 1024


def greet(axis, count, me):
    barrier = pltpu.get_barrier_semaphore()
    for j in range(1, count):
        pl.semaphore_signal(
            barrier, inc=1, device_id={axis: lax.rem(me + j, count)}, device_id_type=MESH
        )
    pl.semaphore_wait(barrier, count - 1)


def causal_kernel(
    devices, per_peer, q_ref, k_ref, v_ref, out_ref, q_all, k_all, v_all, done,
    send_sem, recv_sem, own_sem, back_send, back_recv, back_own,
):
    me = lax.axis_index("seq")
    tokens = q_ref.shape[0]
    width = per_peer * HD
    greet("seq", devices, me)
    pairs = ((q_ref, q_all), (k_ref, k_all), (v_ref, v_all))

    def cols(index):
        return pl.ds(pl.multiple_of(index * width, HD), width)

    own = []
    for a, (src, dst) in enumerate(pairs):
        copy = pltpu.make_async_copy(src.at[:, cols(me)], dst.at[me], own_sem.at[a])
        copy.start()
        own.append(copy)
    sent = []
    for j in range(1, devices):
        peer = lax.rem(me + j, devices)
        for a, (src, dst) in enumerate(pairs):
            copy = pltpu.make_async_remote_copy(
                src_ref=src.at[:, cols(peer)],
                dst_ref=dst.at[me],
                send_sem=send_sem.at[a, j],
                recv_sem=recv_sem.at[a, me],
                device_id={"seq": peer},
                device_id_type=MESH,
            )
            copy.start()
            sent.append(copy)
    for copy in own:
        copy.wait()

    def arrived(dst, sem):
        pltpu.make_async_copy(dst, dst, sem).wait()

    row = lax.broadcasted_iota(jnp.int32, (tokens, tokens), 0)
    col = lax.broadcasted_iota(jnp.int32, (tokens, tokens), 1)
    open_here = col <= row
    for i in range(devices):
        @pl.when(me != i)
        def _(i=i):
            for a, (_, dst) in enumerate(pairs):
                arrived(dst.at[i], recv_sem.at[a, i])

        for h in range(per_peer):
            lanes = slice(h * HD, (h + 1) * HD)
            query = q_all[i, :, lanes]
            last = lax.dot_general(
                query, k_all[i, :, lanes], DOT_T, preferred_element_type=jnp.float32
            ) * (HD ** (-0.5))
            last = jnp.where(open_here, last, masked_score)
            top = jnp.max(last, axis=1, keepdims=True)
            if i:
                keys = k_all[0:i, :, lanes].reshape(i * tokens, HD)
                first = lax.dot_general(
                    query, keys, DOT_T, preferred_element_type=jnp.float32
                ) * (HD ** (-0.5))
                top = jnp.maximum(top, jnp.max(first, axis=1, keepdims=True))
            weights = jnp.where(open_here, jnp.exp(last - top), 0.0)
            total = jnp.sum(weights, axis=1, keepdims=True)
            summed = jnp.dot(
                weights.astype(jnp.bfloat16), v_all[i, :, lanes],
                preferred_element_type=jnp.float32,
            )
            if i:
                weights = jnp.exp(first - top)
                total += jnp.sum(weights, axis=1, keepdims=True)
                values = v_all[0:i, :, lanes].reshape(i * tokens, HD)
                summed += jnp.dot(
                    weights.astype(jnp.bfloat16), values, preferred_element_type=jnp.float32
                )
            done[i, :, lanes] = (summed / total).astype(done.dtype)

        @pl.when(me != i)
        def _(i=i):
            pltpu.make_async_remote_copy(
                src_ref=done.at[i],
                dst_ref=out_ref.at[:, cols(me)],
                send_sem=back_send.at[i],
                recv_sem=back_recv.at[me],
                device_id={"seq": i},
                device_id_type=MESH,
            ).start()

        @pl.when(me == i)
        def _(i=i):
            pltpu.make_async_copy(done.at[i], out_ref.at[:, cols(me)], back_own).start()

    for copy in sent:
        copy.wait_send()
    for i in range(devices):
        @pl.when(me != i)
        def _(i=i):
            arrived(done.at[i], back_send.at[i])
            arrived(out_ref.at[:, cols(i)], back_recv.at[i])

    arrived(out_ref.at[:, cols(me)], back_own)


def exchanged_attention(q, k, v, devices):
    tokens, head_cols = q.shape
    per_peer = head_cols // HD // devices
    width = per_peer * HD
    block = (devices, tokens, width)
    return pl.pallas_call(
        functools.partial(causal_kernel, devices, per_peer),
        name="self_attention",
        out_shape=jax.ShapeDtypeStruct((tokens, head_cols), jnp.bfloat16),
        in_specs=[pl.BlockSpec(memory_space=pl.ANY)] * 3,
        out_specs=pl.BlockSpec(memory_space=pltpu.VMEM),
        scratch_shapes=[pltpu.VMEM(block, jnp.bfloat16)] * 4
        + [
            pltpu.SemaphoreType.DMA((3, devices)),
            pltpu.SemaphoreType.DMA((3, devices)),
            pltpu.SemaphoreType.DMA((3,)),
            pltpu.SemaphoreType.DMA((devices,)),
            pltpu.SemaphoreType.DMA((devices,)),
            pltpu.SemaphoreType.DMA,
        ],
        compiler_params=pltpu.CompilerParams(
            collective_id=0, has_side_effects=True, vmem_limit_bytes=24 * 1024 * 1024
        ),
        cost_estimate=pl.CostEstimate(
            flops=2 * devices * devices * tokens * tokens * width,
            bytes_accessed=200 * 1000 * 1000,
            transcendentals=devices * devices * tokens * tokens * per_peer // 2,
        ),
    )(q, k, v)


def gathered_attention(q_self, k_self, v_self):
    tokens_here, head_cols = q_self.shape
    head_count = head_cols // HD
    query_pos = lax.axis_index("seq") * tokens_here + jnp.arange(tokens_here, dtype=jnp.int32)
    key_part = lax.all_gather(k_self, "seq", axis=0, tiled=True)
    value_part = lax.all_gather(v_self, "seq", axis=0, tiled=True)
    key_count = key_part.shape[0]
    scores = jnp.einsum(
        "qhd,khd->hqk",
        q_self.reshape(tokens_here, head_count, HD),
        key_part.reshape(key_count, head_count, HD),
        preferred_element_type=jnp.float32,
    ) * (HD ** (-0.5))
    key_pos = jnp.arange(key_count, dtype=jnp.int32)
    allowed = (key_pos[None, :] <= query_pos[:, None])[None]
    scores = jnp.where(allowed, scores, masked_score)
    top = jnp.max(scores, axis=2, keepdims=True)
    weights = jnp.where(allowed, jnp.exp(scores - top), 0.0)
    total = jnp.sum(weights, axis=2)
    added = jnp.einsum(
        "hqk,khd->hqd",
        weights.astype(jnp.bfloat16),
        value_part.reshape(key_count, head_count, HD),
        preferred_element_type=jnp.float32,
    )
    out = (added / total[:, :, None]).transpose(1, 0, 2).reshape(tokens_here, head_cols)
    return out.astype(jnp.bfloat16)


def encoder_kernel(
    spans, ids_ref, off_ref, db_ref, gain_ref, query_ref, key_ref, value_ref,
    ctx_ref, part_ref, nbr, sems,
):
    blocks = SET // BLK
    part = part_ref.shape[1]
    lane0 = pl.multiple_of(lax.axis_index("nb") * part, HD)

    def block_copy(i):
        rows = pl.ds(pl.multiple_of(i * BLK, BLK), BLK)
        source = pl.ds(pl.multiple_of(ids_ref[i] * BLK, BLK), BLK)
        return pltpu.make_async_copy(db_ref.at[source], nbr.at[rows], sems.at[i])

    @pl.loop(0, spans * blocks)
    def _(i):
        block_copy(i).start()

    gain = gain_ref[...]
    place = lax.broadcasted_iota(jnp.int32, (SET, SPAN), 1)
    for c in range(spans):
        @pl.loop(c * blocks, (c + 1) * blocks)
        def _(i):
            block_copy(i).wait()

        rows = slice(c * SET, (c + 1) * SET)
        wide = nbr[rows, :].astype(jnp.float32)
        mean = jnp.mean(wide * wide, axis=1, keepdims=True)
        normed = (wide * lax.rsqrt(mean + 1e-06) * gain).astype(jnp.bfloat16)
        eq = (
            jnp.dot(normed, query_ref[...], preferred_element_type=jnp.float32) * (HD ** (-0.5))
        ).astype(jnp.bfloat16)
        part_ref[rows, :] = nbr[rows, pl.ds(lane0, part)]
        keep = place < off_ref[c]
        for h in range(query_ref.shape[1] // HD):
            lanes = slice(h * HD, (h + 1) * HD)
            keys = key_ref[c * SPAN : (c + 1) * SPAN, lanes]
            values = value_ref[c * SPAN : (c + 1) * SPAN, lanes]
            scores = lax.dot_general(
                eq[:, lanes], keys, DOT_T, preferred_element_type=jnp.float32
            )
            scores = jnp.where(keep, scores, masked_score)
            top = jnp.max(scores, axis=1, keepdims=True)
            weights = jnp.where(keep, jnp.exp(scores - top), 0.0)
            total = jnp.sum(weights, axis=1, keepdims=True)
            summed = jnp.dot(
                weights.astype(jnp.bfloat16), values, preferred_element_type=jnp.float32
            )
            ctx_ref[rows, lanes] = (summed / total).astype(jnp.bfloat16)


def encoder_context(ids, offsets, db, gain, query, keys, values, part):
    spans = offsets.shape[0]
    rows = spans * SET
    width = db.shape[1]
    vmem = pl.BlockSpec(memory_space=pltpu.VMEM)
    smem = pl.BlockSpec(memory_space=pltpu.SMEM)
    return pl.pallas_call(
        functools.partial(encoder_kernel, spans),
        name="encoder_context",
        out_shape=(
            jax.ShapeDtypeStruct((rows, query.shape[1]), jnp.bfloat16),
            jax.ShapeDtypeStruct((rows, part), jnp.bfloat16),
        ),
        in_specs=[smem, smem, pl.BlockSpec(memory_space=pl.ANY), vmem, vmem, vmem, vmem],
        out_specs=(vmem, vmem),
        scratch_shapes=[
            pltpu.VMEM((rows, width), jnp.bfloat16),
            pltpu.SemaphoreType.DMA((spans * SET // BLK,)),
        ],
        compiler_params=pltpu.CompilerParams(vmem_limit_bytes=40 * 1024 * 1024),
        cost_estimate=pl.CostEstimate(
            flops=2 * rows * width * query.shape[1],
            bytes_accessed=30 * 1000 * 1000,
            transcendentals=0,
        ),
    )(ids, offsets, db, gain, query, keys, values)


def cross_kernel(
    devices, parts, spans, off_ref, enc_ref, weight_ref, q_ref, next_ref, self_ref, out_ref,
    kv, result, earlier, handed, landed, send_sem, recv_sem,
):
    me = lax.axis_index("seq")
    heads = q_ref.shape[1] // HD
    depth = enc_ref.shape[2]
    greet_next = lax.rem(me + 1, devices)
    barrier = pltpu.get_barrier_semaphore()
    for neighbour in (greet_next, lax.rem(me + devices - 1, devices)):
        pl.semaphore_signal(
            barrier, inc=1, device_id={"seq": neighbour}, device_id_type=MESH
        )
    pl.semaphore_wait(barrier, 2)
    copy = pltpu.make_async_remote_copy(
        src_ref=handed, dst_ref=landed, send_sem=send_sem, recv_sem=recv_sem,
        device_id={"seq": greet_next}, device_id_type=MESH,
    )
    for c in [spans - 1] + list(range(spans - 1)):
        rows = slice(c * SET, (c + 1) * SET)
        total = jnp.dot(
            enc_ref[0, rows, :], weight_ref[0:depth, :], preferred_element_type=jnp.float32
        )
        for n in range(1, parts):
            total += jnp.dot(
                enc_ref[n, rows, :], weight_ref[n * depth : (n + 1) * depth, :],
                preferred_element_type=jnp.float32,
            )
        kv[...] = total.astype(jnp.bfloat16)
        own_rows = slice(c * SPAN, (c + 1) * SPAN)
        for h in range(heads):
            lanes = slice(h * HD, (h + 1) * HD)
            if c == spans - 1:
                after = next_ref[:, lanes]
            else:
                after = q_ref[(c + 1) * SPAN : (c + 2) * SPAN, lanes]
            query = jnp.concatenate([q_ref[own_rows, lanes], after], axis=0)
            scores = lax.dot_general(
                query, kv[:, lanes], DOT_T, preferred_element_type=jnp.float32
            ) * (HD ** (-0.5))
            top = jnp.max(scores, axis=1, keepdims=True)
            weights = jnp.exp(scores - top)
            norm = jnp.sum(weights, axis=1, keepdims=True)
            summed = jnp.dot(
                weights.astype(jnp.bfloat16),
                kv[:, heads * HD + h * HD : heads * HD + (h + 1) * HD],
                preferred_element_type=jnp.float32,
            ) / norm
            result[own_rows, lanes] = summed[:SPAN]
            if c == spans - 1:
                handed[:, lanes] = summed[SPAN:]
            else:
                earlier[(c + 1) * SPAN : (c + 2) * SPAN, lanes] = summed[SPAN:]
        if c == spans - 1:
            copy.start()
    place = lax.broadcasted_iota(jnp.int32, (SPAN, q_ref.shape[1]), 0)
    for c in list(range(1, spans)) + [0]:
        rows = slice(c * SPAN, (c + 1) * SPAN)
        if c == 0:
            copy.wait()
            prior = jnp.where(me == 0, 0.0, landed[...])
        else:
            prior = earlier[rows, :]
        cross = jnp.where(place >= off_ref[c], result[rows, :], prior)
        out_ref[rows, :] = (self_ref[rows, :].astype(jnp.float32) + cross).astype(out_ref.dtype)


def cross_attention(offsets, enc, weight, q, after, self_out, devices):
    parts, rows, depth = enc.shape
    tokens, head_cols = q.shape
    spans = offsets.shape[0]
    vmem = pl.BlockSpec(memory_space=pltpu.VMEM)
    return pl.pallas_call(
        functools.partial(cross_kernel, devices, parts, spans),
        name="cross_attention",
        out_shape=jax.ShapeDtypeStruct((tokens, head_cols), jnp.bfloat16),
        in_specs=[pl.BlockSpec(memory_space=pltpu.SMEM)] + [vmem] * 5,
        out_specs=vmem,
        scratch_shapes=[
            pltpu.VMEM((SET, weight.shape[1]), jnp.bfloat16),
            pltpu.VMEM((tokens, head_cols), jnp.float32),
            pltpu.VMEM((tokens, head_cols), jnp.float32),
            pltpu.VMEM((SPAN, head_cols), jnp.float32),
            pltpu.VMEM((SPAN, head_cols), jnp.float32),
            pltpu.SemaphoreType.DMA,
            pltpu.SemaphoreType.DMA,
        ],
        compiler_params=pltpu.CompilerParams(
            collective_id=1, has_side_effects=True, vmem_limit_bytes=LIMIT
        ),
        cost_estimate=pl.CostEstimate(
            flops=2 * rows * parts * depth * weight.shape[1],
            bytes_accessed=20 * 1000 * 1000,
            transcendentals=0,
        ),
    )(offsets, enc, weight, q, after, self_out)


def own_share(array, axis):
    share = array.shape[axis] // lax.axis_size("nb")
    return lax.dynamic_slice_in_dim(array, lax.axis_index("nb") * share, share, axis)


def local(
    q_self, k_self, v_self, q_cca, memory, database, nbr_block, span_offset,
    enc_query, enc_out, enc_gain, cca_kv,
):
    devices = lax.axis_size("seq")
    owners = lax.axis_size("nb")
    head_cols = q_self.shape[1]
    ids = lax.all_gather(nbr_block, "nb", axis=0, tiled=True)
    db = lax.all_gather(database, "nb", axis=0, tiled=True)
    query_part = lax.all_gather(own_share(enc_query, 1), "seq", axis=0, tiled=True)
    output_part = lax.all_gather(own_share(enc_out, 1), "seq", axis=0, tiled=True)
    after = lax.ppermute(q_cca[:SPAN], "seq", [(i + 1, i) for i in range(devices - 1)])
    if (head_cols // HD) % devices == 0:
        self_out = exchanged_attention(q_self, k_self, v_self, devices)
    else:
        self_out = gathered_attention(q_self, k_self, v_self)
    ctx, nbr_part = encoder_context(
        ids, span_offset, db, enc_gain[None, :], query_part,
        own_share(memory[:, 0], 1), own_share(memory[:, 1], 1), output_part.shape[1],
    )
    ctx_full = lax.all_gather(ctx, "nb", axis=0)
    share = ctx.shape[1]
    update = sum(
        jnp.dot(
            ctx_full[n], output_part[n * share : (n + 1) * share],
            preferred_element_type=jnp.float32,
        )
        for n in range(owners)
    )
    encoded = (nbr_part.astype(jnp.float32) + update).astype(jnp.bfloat16)
    enc_full = lax.all_gather(encoded, "nb", axis=0)
    weight = cca_kv.reshape(cca_kv.shape[0], 2 * head_cols)
    return cross_attention(span_offset, enc_full, weight, q_cca, after, self_out, devices)


def solution(mesh):
    in_specs = (
        P("seq", "nb"),
        P("seq", "nb"),
        P("seq", "nb"),
        P("seq", "nb"),
        P("seq", None, None),
        P(("seq", "nb"), None),
        P(("seq", "nb")),
        P("seq"),
        P("seq", None),
        P("seq", None),
        P(),
        P(None, None, "nb"),
    )
    out_specs = P("seq", "nb")
    return jax.shard_map(local, mesh=mesh, in_specs=in_specs, out_specs=out_specs, check_vma=False)
```

```python
import functools

import jax
import jax.numpy as jnp
from jax import lax
from jax.experimental import pallas as pl
from jax.experimental.pallas import tpu as pltpu
from jax.sharding import PartitionSpec as P

HD = 128
SPAN = 64
K = 2
R = 128
BLK = 16
SET = K * R

masked_score = -1e30
MESH = pl.DeviceIdType.MESH
DOT_T = (((1,), (1,)), ((), ()))
LIMIT = 56 * 1024 * 1024


CORES = 2


class Group:
    def __init__(self, count):
        self.count = count
        self.me = lax.axis_index("nb")
        self.partner = self.me + 1 - 2 * lax.rem(self.me, CORES)
        self.chips = count // CORES

    def far(self, j, of=None):
        return lax.rem((self.me if of is None else of) + CORES * j, self.count)

    def targets(self):
        return [self.partner] + [self.far(j) for j in range(1, self.chips)]

    def share(self, slot_ref, source, send_sem, recv_sem):
        copies = []
        for t, peer in enumerate(self.targets()):
            copy = pltpu.make_async_remote_copy(
                src_ref=source, dst_ref=slot_ref(self.me), send_sem=send_sem(t),
                recv_sem=recv_sem(self.me), device_id={"nb": peer}, device_id_type=MESH,
            )
            copy.start()
            copies.append(copy)
        return copies

    def pass_on(self, slot_ref, send_sem, recv_sem):
        copies = []
        for j in range(1, self.chips):
            slot = self.far(j)
            arrived(slot_ref(slot), recv_sem(slot))
            copy = pltpu.make_async_remote_copy(
                src_ref=slot_ref(slot), dst_ref=slot_ref(slot),
                send_sem=send_sem(self.chips + j - 1), recv_sem=recv_sem(slot),
                device_id={"nb": self.partner}, device_id_type=MESH,
            )
            copy.start()
            copies.append(copy)
        return copies

    def finish(self, slot_ref, recv_sem):
        for j in range(self.chips):
            slot = self.far(j, self.partner)
            arrived(slot_ref(slot), recv_sem(slot))


def arrived(dst, sem):
    pltpu.make_async_copy(dst, dst, sem).wait()


def greet(targets):
    barrier = pltpu.get_barrier_semaphore()
    for target in targets:
        pl.semaphore_signal(barrier, inc=1, device_id=target, device_id_type=MESH)
    pl.semaphore_wait(barrier, len(targets))


def causal_kernel(
    devices, owners, per_peer, q_ref, k_ref, v_ref, db_ref, out_ref, db_out, q_all, k_all, v_all,
    done, send_sem, recv_sem, own_sem, back_send, back_recv, back_own, db_send, db_recv, db_own,
):
    me = lax.axis_index("seq")
    tokens = q_ref.shape[0]
    width = per_peer * HD
    group = Group(owners)
    greet(
        [{"seq": lax.rem(me + j, devices)} for j in range(1, devices)]
        + [{"nb": peer} for peer in group.targets()]
    )
    pairs = ((q_ref, q_all), (k_ref, k_all), (v_ref, v_all))

    def cols(index):
        return pl.ds(pl.multiple_of(index * width, HD), width)

    own = []
    for a, (src, dst) in enumerate(pairs):
        copy = pltpu.make_async_copy(src.at[:, cols(me)], dst.at[me], own_sem.at[a])
        copy.start()
        own.append(copy)
    sent = []
    for j in range(1, devices):
        peer = lax.rem(me + j, devices)
        for a, (src, dst) in enumerate(pairs):
            copy = pltpu.make_async_remote_copy(
                src_ref=src.at[:, cols(peer)],
                dst_ref=dst.at[me],
                send_sem=send_sem.at[a, j],
                recv_sem=recv_sem.at[a, me],
                device_id={"seq": peer},
                device_id_type=MESH,
            )
            copy.start()
            sent.append(copy)
    db_slot = lambda slot: db_out.at[slot]
    db_sems = (lambda t: db_send.at[t], lambda slot: db_recv.at[slot])
    db_copies = group.share(db_slot, db_ref, *db_sems)
    own_db = pltpu.make_async_copy(db_ref, db_slot(group.me), db_own)
    own_db.start()
    for copy in own:
        copy.wait()

    row = lax.broadcasted_iota(jnp.int32, (tokens, tokens), 0)
    col = lax.broadcasted_iota(jnp.int32, (tokens, tokens), 1)
    open_here = col <= row
    for i in range(devices):
        @pl.when(me != i)
        def _(i=i):
            for a, (_, dst) in enumerate(pairs):
                arrived(dst.at[i], recv_sem.at[a, i])

        for h in range(per_peer):
            lanes = slice(h * HD, (h + 1) * HD)
            query = q_all[i, :, lanes]
            last = lax.dot_general(
                query, k_all[i, :, lanes], DOT_T, preferred_element_type=jnp.float32
            ) * (HD ** (-0.5))
            last = jnp.where(open_here, last, masked_score)
            top = jnp.max(last, axis=1, keepdims=True)
            if i:
                keys = k_all[0:i, :, lanes].reshape(i * tokens, HD)
                first = lax.dot_general(
                    query, keys, DOT_T, preferred_element_type=jnp.float32
                ) * (HD ** (-0.5))
                top = jnp.maximum(top, jnp.max(first, axis=1, keepdims=True))
            weights = jnp.where(open_here, jnp.exp(last - top), 0.0)
            total = jnp.sum(weights, axis=1, keepdims=True)
            summed = jnp.dot(
                weights.astype(jnp.bfloat16), v_all[i, :, lanes],
                preferred_element_type=jnp.float32,
            )
            if i:
                weights = jnp.exp(first - top)
                total += jnp.sum(weights, axis=1, keepdims=True)
                values = v_all[0:i, :, lanes].reshape(i * tokens, HD)
                summed += jnp.dot(
                    weights.astype(jnp.bfloat16), values, preferred_element_type=jnp.float32
                )
            done[i, :, lanes] = (summed / total).astype(done.dtype)

        @pl.when(me != i)
        def _(i=i):
            pltpu.make_async_remote_copy(
                src_ref=done.at[i],
                dst_ref=out_ref.at[:, cols(me)],
                send_sem=back_send.at[i],
                recv_sem=back_recv.at[me],
                device_id={"seq": i},
                device_id_type=MESH,
            ).start()

        @pl.when(me == i)
        def _(i=i):
            pltpu.make_async_copy(done.at[i], out_ref.at[:, cols(me)], back_own).start()

        if i == devices // 2:
            db_copies += group.pass_on(db_slot, *db_sems)

    own_db.wait()
    group.finish(db_slot, db_sems[1])
    for copy in sent + db_copies:
        copy.wait_send()
    for i in range(devices):
        @pl.when(me != i)
        def _(i=i):
            arrived(done.at[i], back_send.at[i])
            arrived(out_ref.at[:, cols(i)], back_recv.at[i])

    arrived(out_ref.at[:, cols(me)], back_own)


def exchanged_attention(q, k, v, db, devices, owners):
    tokens, head_cols = q.shape
    per_peer = head_cols // HD // devices
    width = per_peer * HD
    block = (devices, tokens, width)
    return pl.pallas_call(
        functools.partial(causal_kernel, devices, owners, per_peer),
        name="self_attention",
        out_shape=(
            jax.ShapeDtypeStruct((tokens, head_cols), jnp.bfloat16),
            jax.ShapeDtypeStruct((owners,) + db.shape, db.dtype),
        ),
        in_specs=[pl.BlockSpec(memory_space=pl.ANY)] * 4,
        out_specs=(pl.BlockSpec(memory_space=pltpu.VMEM), pl.BlockSpec(memory_space=pl.ANY)),
        scratch_shapes=[pltpu.VMEM(block, jnp.bfloat16)] * 4
        + [
            pltpu.SemaphoreType.DMA((3, devices)),
            pltpu.SemaphoreType.DMA((3, devices)),
            pltpu.SemaphoreType.DMA((3,)),
            pltpu.SemaphoreType.DMA((devices,)),
            pltpu.SemaphoreType.DMA((devices,)),
            pltpu.SemaphoreType.DMA,
            pltpu.SemaphoreType.DMA((owners,)),
            pltpu.SemaphoreType.DMA((owners,)),
            pltpu.SemaphoreType.DMA,
        ],
        compiler_params=pltpu.CompilerParams(
            collective_id=0, has_side_effects=True, vmem_limit_bytes=24 * 1024 * 1024
        ),
        cost_estimate=pl.CostEstimate(
            flops=2 * devices * devices * tokens * tokens * width,
            bytes_accessed=200 * 1000 * 1000,
            transcendentals=devices * devices * tokens * tokens * per_peer // 2,
        ),
    )(q, k, v, db)


def gathered_attention(q_self, k_self, v_self):
    tokens_here, head_cols = q_self.shape
    head_count = head_cols // HD
    query_pos = lax.axis_index("seq") * tokens_here + jnp.arange(tokens_here, dtype=jnp.int32)
    key_part = lax.all_gather(k_self, "seq", axis=0, tiled=True)
    value_part = lax.all_gather(v_self, "seq", axis=0, tiled=True)
    key_count = key_part.shape[0]
    scores = jnp.einsum(
        "qhd,khd->hqk",
        q_self.reshape(tokens_here, head_count, HD),
        key_part.reshape(key_count, head_count, HD),
        preferred_element_type=jnp.float32,
    ) * (HD ** (-0.5))
    key_pos = jnp.arange(key_count, dtype=jnp.int32)
    allowed = (key_pos[None, :] <= query_pos[:, None])[None]
    scores = jnp.where(allowed, scores, masked_score)
    top = jnp.max(scores, axis=2, keepdims=True)
    weights = jnp.where(allowed, jnp.exp(scores - top), 0.0)
    total = jnp.sum(weights, axis=2)
    added = jnp.einsum(
        "hqk,khd->hqd",
        weights.astype(jnp.bfloat16),
        value_part.reshape(key_count, head_count, HD),
        preferred_element_type=jnp.float32,
    )
    out = (added / total[:, :, None]).transpose(1, 0, 2).reshape(tokens_here, head_cols)
    return out.astype(jnp.bfloat16)


def encoder_kernel(
    spans, ids_ref, off_ref, db_ref, gain_ref, query_ref, key_ref, value_ref,
    ctx_ref, part_ref, nbr, sems,
):
    blocks = SET // BLK
    part = part_ref.shape[1]
    lane0 = pl.multiple_of(lax.axis_index("nb") * part, HD)

    def block_copy(i):
        rows = pl.ds(pl.multiple_of(i * BLK, BLK), BLK)
        source = pl.ds(pl.multiple_of(ids_ref[i] * BLK, BLK), BLK)
        return pltpu.make_async_copy(db_ref.at[source], nbr.at[rows], sems.at[i])

    @pl.loop(0, spans * blocks)
    def _(i):
        block_copy(i).start()

    gain = gain_ref[...]
    place = lax.broadcasted_iota(jnp.int32, (SET, SPAN), 1)
    for c in range(spans):
        @pl.loop(c * blocks, (c + 1) * blocks)
        def _(i):
            block_copy(i).wait()

        rows = slice(c * SET, (c + 1) * SET)
        wide = nbr[rows, :].astype(jnp.float32)
        mean = jnp.mean(wide * wide, axis=1, keepdims=True)
        normed = (wide * lax.rsqrt(mean + 1e-06) * gain).astype(jnp.bfloat16)
        eq = (
            jnp.dot(normed, query_ref[...], preferred_element_type=jnp.float32) * (HD ** (-0.5))
        ).astype(jnp.bfloat16)
        part_ref[rows, :] = nbr[rows, pl.ds(lane0, part)]
        keep = place < off_ref[c]
        for h in range(query_ref.shape[1] // HD):
            lanes = slice(h * HD, (h + 1) * HD)
            keys = key_ref[c * SPAN : (c + 1) * SPAN, lanes]
            values = value_ref[c * SPAN : (c + 1) * SPAN, lanes]
            scores = lax.dot_general(
                eq[:, lanes], keys, DOT_T, preferred_element_type=jnp.float32
            )
            scores = jnp.where(keep, scores, masked_score)
            top = jnp.max(scores, axis=1, keepdims=True)
            weights = jnp.where(keep, jnp.exp(scores - top), 0.0)
            total = jnp.sum(weights, axis=1, keepdims=True)
            summed = jnp.dot(
                weights.astype(jnp.bfloat16), values, preferred_element_type=jnp.float32
            )
            ctx_ref[rows, lanes] = (summed / total).astype(jnp.bfloat16)


def encoder_context(ids, offsets, db, gain, query, keys, values, part):
    spans = offsets.shape[0]
    rows = spans * SET
    width = db.shape[1]
    vmem = pl.BlockSpec(memory_space=pltpu.VMEM)
    smem = pl.BlockSpec(memory_space=pltpu.SMEM)
    return pl.pallas_call(
        functools.partial(encoder_kernel, spans),
        name="encoder_context",
        out_shape=(
            jax.ShapeDtypeStruct((rows, query.shape[1]), jnp.bfloat16),
            jax.ShapeDtypeStruct((rows, part), jnp.bfloat16),
        ),
        in_specs=[smem, smem, pl.BlockSpec(memory_space=pl.ANY), vmem, vmem, vmem, vmem],
        out_specs=(vmem, vmem),
        scratch_shapes=[
            pltpu.VMEM((rows, width), jnp.bfloat16),
            pltpu.SemaphoreType.DMA((spans * SET // BLK,)),
        ],
        compiler_params=pltpu.CompilerParams(vmem_limit_bytes=40 * 1024 * 1024),
        cost_estimate=pl.CostEstimate(
            flops=2 * rows * width * query.shape[1],
            bytes_accessed=30 * 1000 * 1000,
            transcendentals=0,
        ),
    )(ids, offsets, db, gain, query, keys, values)


def cross_kernel(
    devices, parts, spans, off_ref, ctx_ref, outw_ref, nbr_ref, weight_ref, q_ref, next_ref,
    self_ref, out_ref, enc_ref, kv, result, earlier, handed, landed, send_sem, recv_sem,
    enc_send, enc_recv,
):
    me = lax.axis_index("seq")
    heads = q_ref.shape[1] // HD
    depth = enc_ref.shape[2]
    share = ctx_ref.shape[2]
    greet_next = lax.rem(me + 1, devices)
    group = Group(parts)
    greet(
        [{"seq": greet_next}, {"seq": lax.rem(me + devices - 1, devices)}]
        + [{"nb": peer} for peer in group.targets()]
    )
    order = [spans - 1] + list(range(spans - 1))
    enc_copies = []

    def wiring(c):
        rows = pl.ds(c * SET, SET)
        return (
            lambda slot: enc_ref.at[slot, rows],
            lambda t: enc_send.at[t, c],
            lambda slot: enc_recv.at[slot, c],
        )

    for c in order:
        rows = slice(c * SET, (c + 1) * SET)
        total = nbr_ref[rows, :].astype(jnp.float32)
        update = jnp.dot(
            ctx_ref[0, rows, :], outw_ref[0:share, :], preferred_element_type=jnp.float32
        )
        for n in range(1, parts):
            update += jnp.dot(
                ctx_ref[n, rows, :], outw_ref[n * share : (n + 1) * share, :],
                preferred_element_type=jnp.float32,
            )
        enc_ref[group.me, rows, :] = (total + update).astype(jnp.bfloat16)
        slot_ref, sends, recvs = wiring(c)
        enc_copies += group.share(slot_ref, slot_ref(group.me), sends, recvs)
    copy = pltpu.make_async_remote_copy(
        src_ref=handed, dst_ref=landed, send_sem=send_sem, recv_sem=recv_sem,
        device_id={"seq": greet_next}, device_id_type=MESH,
    )
    for c in order:
        rows = slice(c * SET, (c + 1) * SET)
        slot_ref, sends, recvs = wiring(c)
        enc_copies += group.pass_on(slot_ref, sends, recvs)
        group.finish(slot_ref, recvs)
        total = jnp.dot(
            enc_ref[0, rows, :], weight_ref[0:depth, :], preferred_element_type=jnp.float32
        )
        for n in range(1, parts):
            total += jnp.dot(
                enc_ref[n, rows, :], weight_ref[n * depth : (n + 1) * depth, :],
                preferred_element_type=jnp.float32,
            )
        kv[...] = total.astype(jnp.bfloat16)
        own_rows = slice(c * SPAN, (c + 1) * SPAN)
        for h in range(heads):
            lanes = slice(h * HD, (h + 1) * HD)
            if c == spans - 1:
                after = next_ref[:, lanes]
            else:
                after = q_ref[(c + 1) * SPAN : (c + 2) * SPAN, lanes]
            query = jnp.concatenate([q_ref[own_rows, lanes], after], axis=0)
            scores = lax.dot_general(
                query, kv[:, lanes], DOT_T, preferred_element_type=jnp.float32
            ) * (HD ** (-0.5))
            top = jnp.max(scores, axis=1, keepdims=True)
            weights = jnp.exp(scores - top)
            norm = jnp.sum(weights, axis=1, keepdims=True)
            summed = jnp.dot(
                weights.astype(jnp.bfloat16),
                kv[:, heads * HD + h * HD : heads * HD + (h + 1) * HD],
                preferred_element_type=jnp.float32,
            ) / norm
            result[own_rows, lanes] = summed[:SPAN]
            if c == spans - 1:
                handed[:, lanes] = summed[SPAN:]
            else:
                earlier[(c + 1) * SPAN : (c + 2) * SPAN, lanes] = summed[SPAN:]
        if c == spans - 1:
            copy.start()
    place = lax.broadcasted_iota(jnp.int32, (SPAN, q_ref.shape[1]), 0)
    for c in list(range(1, spans)) + [0]:
        rows = slice(c * SPAN, (c + 1) * SPAN)
        if c == 0:
            copy.wait()
            prior = jnp.where(me == 0, 0.0, landed[...])
        else:
            prior = earlier[rows, :]
        cross = jnp.where(place >= off_ref[c], result[rows, :], prior)
        out_ref[rows, :] = (self_ref[rows, :].astype(jnp.float32) + cross).astype(out_ref.dtype)
    for copy in enc_copies:
        copy.wait_send()


def cross_attention(offsets, ctx, output_part, nbr_part, weight, q, after, self_out, devices):
    parts = ctx.shape[0]
    rows, depth = nbr_part.shape
    tokens, head_cols = q.shape
    spans = offsets.shape[0]
    vmem = pl.BlockSpec(memory_space=pltpu.VMEM)
    return pl.pallas_call(
        functools.partial(cross_kernel, devices, parts, spans),
        name="cross_attention",
        out_shape=jax.ShapeDtypeStruct((tokens, head_cols), jnp.bfloat16),
        in_specs=[pl.BlockSpec(memory_space=pltpu.SMEM)] + [vmem] * 7,
        out_specs=vmem,
        scratch_shapes=[
            pltpu.VMEM((parts, rows, depth), jnp.bfloat16),
            pltpu.VMEM((SET, weight.shape[1]), jnp.bfloat16),
            pltpu.VMEM((tokens, head_cols), jnp.float32),
            pltpu.VMEM((tokens, head_cols), jnp.float32),
            pltpu.VMEM((SPAN, head_cols), jnp.float32),
            pltpu.VMEM((SPAN, head_cols), jnp.float32),
            pltpu.SemaphoreType.DMA,
            pltpu.SemaphoreType.DMA,
            pltpu.SemaphoreType.DMA((parts, spans)),
            pltpu.SemaphoreType.DMA((parts, spans)),
        ],
        compiler_params=pltpu.CompilerParams(
            collective_id=1, has_side_effects=True, vmem_limit_bytes=LIMIT
        ),
        cost_estimate=pl.CostEstimate(
            flops=2 * rows * parts * depth * weight.shape[1],
            bytes_accessed=20 * 1000 * 1000,
            transcendentals=0,
        ),
    )(offsets, ctx, output_part, nbr_part, weight, q, after, self_out)


def own_share(array, axis):
    share = array.shape[axis] // lax.axis_size("nb")
    return lax.dynamic_slice_in_dim(array, lax.axis_index("nb") * share, share, axis)


def local(
    q_self, k_self, v_self, q_cca, memory, database, nbr_block, span_offset,
    enc_query, enc_out, enc_gain, cca_kv,
):
    devices = lax.axis_size("seq")
    owners = lax.axis_size("nb")
    head_cols = q_self.shape[1]
    ids = lax.all_gather(nbr_block, "nb", axis=0, tiled=True)
    query_part = lax.all_gather(own_share(enc_query, 1), "seq", axis=0, tiled=True)
    output_part = lax.all_gather(own_share(enc_out, 1), "seq", axis=0, tiled=True)
    after = lax.ppermute(q_cca[:SPAN], "seq", [(i + 1, i) for i in range(devices - 1)])
    if (head_cols // HD) % devices == 0:
        self_out, db = exchanged_attention(q_self, k_self, v_self, database, devices, owners)
        db = db.reshape(-1, database.shape[1])
    else:
        db = lax.all_gather(database, "nb", axis=0, tiled=True)
        self_out = gathered_attention(q_self, k_self, v_self)
    ctx, nbr_part = encoder_context(
        ids, span_offset, db, enc_gain[None, :], query_part,
        own_share(memory[:, 0], 1), own_share(memory[:, 1], 1), output_part.shape[1],
    )
    ctx_full = lax.all_gather(ctx, "nb", axis=0)
    weight = cca_kv.reshape(cca_kv.shape[0], 2 * head_cols)
    return cross_attention(
        span_offset, ctx_full, output_part, nbr_part, weight, q_cca, after, self_out, devices
    )


def solution(mesh):
    in_specs = (
        P("seq", "nb"),
        P("seq", "nb"),
        P("seq", "nb"),
        P("seq", "nb"),
        P("seq", None, None),
        P(("seq", "nb"), None),
        P(("seq", "nb")),
        P("seq"),
        P("seq", None),
        P("seq", None),
        P(),
        P(None, None, "nb"),
    )
    out_specs = P("seq", "nb")
    return jax.shard_map(local, mesh=mesh, in_specs=in_specs, out_specs=out_specs, check_vma=False)
```

```python
import functools

import jax
import jax.numpy as jnp
from jax import lax
from jax.experimental import pallas as pl
from jax.experimental.pallas import tpu as pltpu
from jax.sharding import PartitionSpec as P

HD = 128
SPAN = 64
K = 2
R = 128
BLK = 16
SET = K * R

masked_score = -1e30
MESH = pl.DeviceIdType.MESH
DOT_T = (((1,), (1,)), ((), ()))
LIMIT = 56 * 1024 * 1024


CORES = 2


class Group:
    def __init__(self, count):
        self.count = count
        self.me = lax.axis_index("nb")
        self.partner = self.me + 1 - 2 * lax.rem(self.me, CORES)
        self.chips = count // CORES

    def far(self, j, of=None):
        return lax.rem((self.me if of is None else of) + CORES * j, self.count)

    def targets(self):
        return [self.partner] + [self.far(j) for j in range(1, self.chips)]

    def share(self, slot_ref, source, send_sem, recv_sem):
        copies = []
        for t, peer in enumerate(self.targets()):
            copy = pltpu.make_async_remote_copy(
                src_ref=source, dst_ref=slot_ref(self.me), send_sem=send_sem(t),
                recv_sem=recv_sem(self.me), device_id={"nb": peer}, device_id_type=MESH,
            )
            copy.start()
            copies.append(copy)
        return copies

    def pass_on(self, slot_ref, send_sem, recv_sem):
        copies = []
        for j in range(1, self.chips):
            slot = self.far(j)
            arrived(slot_ref(slot), recv_sem(slot))
            copy = pltpu.make_async_remote_copy(
                src_ref=slot_ref(slot), dst_ref=slot_ref(slot),
                send_sem=send_sem(self.chips + j - 1), recv_sem=recv_sem(slot),
                device_id={"nb": self.partner}, device_id_type=MESH,
            )
            copy.start()
            copies.append(copy)
        return copies

    def finish(self, slot_ref, recv_sem):
        for j in range(self.chips):
            slot = self.far(j, self.partner)
            arrived(slot_ref(slot), recv_sem(slot))


def arrived(dst, sem):
    pltpu.make_async_copy(dst, dst, sem).wait()


def greet(targets):
    barrier = pltpu.get_barrier_semaphore()
    for target in targets:
        pl.semaphore_signal(barrier, inc=1, device_id=target, device_id_type=MESH)
    pl.semaphore_wait(barrier, len(targets))


def causal_kernel(
    devices, owners, per_peer, q_ref, k_ref, v_ref, db_ref, out_ref, db_out, q_all, k_all, v_all,
    done, send_sem, recv_sem, own_sem, back_send, back_recv, back_own, db_send, db_recv, db_own,
):
    me = lax.axis_index("seq")
    tokens = q_ref.shape[0]
    width = per_peer * HD
    group = Group(owners)
    greet(
        [{"seq": lax.rem(me + j, devices)} for j in range(1, devices)]
        + [{"nb": peer} for peer in group.targets()]
    )
    pairs = ((q_ref, q_all), (k_ref, k_all), (v_ref, v_all))

    def cols(index):
        return pl.ds(pl.multiple_of(index * width, HD), width)

    own = []
    for a, (src, dst) in enumerate(pairs):
        copy = pltpu.make_async_copy(src.at[:, cols(me)], dst.at[me], own_sem.at[a])
        copy.start()
        own.append(copy)
    sent = []
    for j in range(1, devices):
        peer = lax.rem(me + j, devices)
        for a, (src, dst) in enumerate(pairs):
            copy = pltpu.make_async_remote_copy(
                src_ref=src.at[:, cols(peer)],
                dst_ref=dst.at[me],
                send_sem=send_sem.at[a, j],
                recv_sem=recv_sem.at[a, me],
                device_id={"seq": peer},
                device_id_type=MESH,
            )
            copy.start()
            sent.append(copy)
    db_slot = lambda slot: db_out.at[slot]
    db_sems = (lambda t: db_send.at[t], lambda slot: db_recv.at[slot])
    db_copies = group.share(db_slot, db_ref, *db_sems)
    own_db = pltpu.make_async_copy(db_ref, db_slot(group.me), db_own)
    own_db.start()
    for copy in own:
        copy.wait()

    row = lax.broadcasted_iota(jnp.int32, (tokens, tokens), 0)
    col = lax.broadcasted_iota(jnp.int32, (tokens, tokens), 1)
    open_here = col <= row
    for i in range(devices):
        @pl.when(me != i)
        def _(i=i):
            for a, (_, dst) in enumerate(pairs):
                arrived(dst.at[i], recv_sem.at[a, i])

        for h in range(per_peer):
            lanes = slice(h * HD, (h + 1) * HD)
            query = q_all[i, :, lanes]
            last = lax.dot_general(
                query, k_all[i, :, lanes], DOT_T, preferred_element_type=jnp.float32
            ) * (HD ** (-0.5))
            last = jnp.where(open_here, last, masked_score)
            top = jnp.max(last, axis=1, keepdims=True)
            if i:
                keys = k_all[0:i, :, lanes].reshape(i * tokens, HD)
                first = lax.dot_general(
                    query, keys, DOT_T, preferred_element_type=jnp.float32
                ) * (HD ** (-0.5))
                top = jnp.maximum(top, jnp.max(first, axis=1, keepdims=True))
            weights = jnp.where(open_here, jnp.exp(last - top), 0.0)
            total = jnp.sum(weights, axis=1, keepdims=True)
            summed = jnp.dot(
                weights.astype(jnp.bfloat16), v_all[i, :, lanes],
                preferred_element_type=jnp.float32,
            )
            if i:
                weights = jnp.exp(first - top)
                total += jnp.sum(weights, axis=1, keepdims=True)
                values = v_all[0:i, :, lanes].reshape(i * tokens, HD)
                summed += jnp.dot(
                    weights.astype(jnp.bfloat16), values, preferred_element_type=jnp.float32
                )
            done[i, :, lanes] = (summed / total).astype(done.dtype)

        @pl.when(me != i)
        def _(i=i):
            pltpu.make_async_remote_copy(
                src_ref=done.at[i],
                dst_ref=out_ref.at[:, cols(me)],
                send_sem=back_send.at[i],
                recv_sem=back_recv.at[me],
                device_id={"seq": i},
                device_id_type=MESH,
            ).start()

        @pl.when(me == i)
        def _(i=i):
            pltpu.make_async_copy(done.at[i], out_ref.at[:, cols(me)], back_own).start()

        if i == devices // 2:
            db_copies += group.pass_on(db_slot, *db_sems)

    own_db.wait()
    group.finish(db_slot, db_sems[1])
    for copy in sent + db_copies:
        copy.wait_send()
    for i in range(devices):
        @pl.when(me != i)
        def _(i=i):
            arrived(done.at[i], back_send.at[i])
            arrived(out_ref.at[:, cols(i)], back_recv.at[i])

    arrived(out_ref.at[:, cols(me)], back_own)


def exchanged_attention(q, k, v, db, devices, owners):
    tokens, head_cols = q.shape
    per_peer = head_cols // HD // devices
    width = per_peer * HD
    block = (devices, tokens, width)
    return pl.pallas_call(
        functools.partial(causal_kernel, devices, owners, per_peer),
        name="self_attention",
        out_shape=(
            jax.ShapeDtypeStruct((tokens, head_cols), jnp.bfloat16),
            jax.ShapeDtypeStruct((owners,) + db.shape, db.dtype),
        ),
        in_specs=[pl.BlockSpec(memory_space=pl.ANY)] * 4,
        out_specs=(pl.BlockSpec(memory_space=pltpu.VMEM), pl.BlockSpec(memory_space=pl.ANY)),
        scratch_shapes=[pltpu.VMEM(block, jnp.bfloat16)] * 4
        + [
            pltpu.SemaphoreType.DMA((3, devices)),
            pltpu.SemaphoreType.DMA((3, devices)),
            pltpu.SemaphoreType.DMA((3,)),
            pltpu.SemaphoreType.DMA((devices,)),
            pltpu.SemaphoreType.DMA((devices,)),
            pltpu.SemaphoreType.DMA,
            pltpu.SemaphoreType.DMA((owners,)),
            pltpu.SemaphoreType.DMA((owners,)),
            pltpu.SemaphoreType.DMA,
        ],
        compiler_params=pltpu.CompilerParams(
            collective_id=0, has_side_effects=True, vmem_limit_bytes=LIMIT
        ),
        cost_estimate=pl.CostEstimate(
            flops=2 * devices * devices * tokens * tokens * width,
            bytes_accessed=200 * 1000 * 1000,
            transcendentals=devices * devices * tokens * tokens * per_peer // 2,
        ),
    )(q, k, v, db)


def gathered_attention(q_self, k_self, v_self):
    tokens_here, head_cols = q_self.shape
    head_count = head_cols // HD
    query_pos = lax.axis_index("seq") * tokens_here + jnp.arange(tokens_here, dtype=jnp.int32)
    key_part = lax.all_gather(k_self, "seq", axis=0, tiled=True)
    value_part = lax.all_gather(v_self, "seq", axis=0, tiled=True)
    key_count = key_part.shape[0]
    scores = jnp.einsum(
        "qhd,khd->hqk",
        q_self.reshape(tokens_here, head_count, HD),
        key_part.reshape(key_count, head_count, HD),
        preferred_element_type=jnp.float32,
    ) * (HD ** (-0.5))
    key_pos = jnp.arange(key_count, dtype=jnp.int32)
    allowed = (key_pos[None, :] <= query_pos[:, None])[None]
    scores = jnp.where(allowed, scores, masked_score)
    top = jnp.max(scores, axis=2, keepdims=True)
    weights = jnp.where(allowed, jnp.exp(scores - top), 0.0)
    total = jnp.sum(weights, axis=2)
    added = jnp.einsum(
        "hqk,khd->hqd",
        weights.astype(jnp.bfloat16),
        value_part.reshape(key_count, head_count, HD),
        preferred_element_type=jnp.float32,
    )
    out = (added / total[:, :, None]).transpose(1, 0, 2).reshape(tokens_here, head_cols)
    return out.astype(jnp.bfloat16)


def encoder_kernel(
    spans, ids_ref, off_ref, db_ref, gain_ref, query_ref, key_ref, value_ref,
    ctx_ref, part_ref, nbr, sems,
):
    blocks = SET // BLK
    part = part_ref.shape[1]
    lane0 = pl.multiple_of(lax.axis_index("nb") * part, HD)

    def block_copy(i):
        rows = pl.ds(pl.multiple_of(i * BLK, BLK), BLK)
        source = pl.ds(pl.multiple_of(ids_ref[i] * BLK, BLK), BLK)
        return pltpu.make_async_copy(db_ref.at[source], nbr.at[rows], sems.at[i])

    @pl.loop(0, spans * blocks)
    def _(i):
        block_copy(i).start()

    gain = gain_ref[...]
    place = lax.broadcasted_iota(jnp.int32, (SET, SPAN), 1)
    for c in range(spans):
        @pl.loop(c * blocks, (c + 1) * blocks)
        def _(i):
            block_copy(i).wait()

        rows = slice(c * SET, (c + 1) * SET)
        wide = nbr[rows, :].astype(jnp.float32)
        mean = jnp.mean(wide * wide, axis=1, keepdims=True)
        normed = (wide * lax.rsqrt(mean + 1e-06) * gain).astype(jnp.bfloat16)
        eq = (
            jnp.dot(normed, query_ref[...], preferred_element_type=jnp.float32) * (HD ** (-0.5))
        ).astype(jnp.bfloat16)
        part_ref[rows, :] = nbr[rows, pl.ds(lane0, part)]
        keep = place < off_ref[c]
        for h in range(query_ref.shape[1] // HD):
            lanes = slice(h * HD, (h + 1) * HD)
            keys = key_ref[c * SPAN : (c + 1) * SPAN, lanes]
            values = value_ref[c * SPAN : (c + 1) * SPAN, lanes]
            scores = lax.dot_general(
                eq[:, lanes], keys, DOT_T, preferred_element_type=jnp.float32
            )
            scores = jnp.where(keep, scores, masked_score)
            top = jnp.max(scores, axis=1, keepdims=True)
            weights = jnp.where(keep, jnp.exp(scores - top), 0.0)
            total = jnp.sum(weights, axis=1, keepdims=True)
            summed = jnp.dot(
                weights.astype(jnp.bfloat16), values, preferred_element_type=jnp.float32
            )
            ctx_ref[rows, lanes] = (summed / total).astype(jnp.bfloat16)


def encoder_context(ids, offsets, db, gain, query, keys, values, part):
    spans = offsets.shape[0]
    rows = spans * SET
    width = db.shape[1]
    vmem = pl.BlockSpec(memory_space=pltpu.VMEM)
    smem = pl.BlockSpec(memory_space=pltpu.SMEM)
    return pl.pallas_call(
        functools.partial(encoder_kernel, spans),
        name="encoder_context",
        out_shape=(
            jax.ShapeDtypeStruct((rows, query.shape[1]), jnp.bfloat16),
            jax.ShapeDtypeStruct((rows, part), jnp.bfloat16),
        ),
        in_specs=[smem, smem, pl.BlockSpec(memory_space=pl.ANY), vmem, vmem, vmem, vmem],
        out_specs=(vmem, vmem),
        scratch_shapes=[
            pltpu.VMEM((rows, width), jnp.bfloat16),
            pltpu.SemaphoreType.DMA((spans * SET // BLK,)),
        ],
        compiler_params=pltpu.CompilerParams(vmem_limit_bytes=LIMIT),
        cost_estimate=pl.CostEstimate(
            flops=2 * rows * width * query.shape[1],
            bytes_accessed=30 * 1000 * 1000,
            transcendentals=0,
        ),
    )(ids, offsets, db, gain, query, keys, values)


def gather_kernel(owners, chunks, src_ref, out_ref, send_sem, recv_sem, own_sem):
    group = Group(owners)
    greet([{"nb": peer} for peer in group.targets()])
    own = pltpu.make_async_copy(src_ref, out_ref.at[group.me], own_sem)
    own.start()
    size = src_ref.shape[0] // chunks

    def wiring(c):
        rows = pl.ds(c * size, size)
        return (
            lambda slot: out_ref.at[slot, rows],
            lambda t: send_sem.at[t, c],
            lambda slot: recv_sem.at[slot, c],
        )

    copies = []
    for c in range(chunks):
        slot_ref, sends, recvs = wiring(c)
        copies += group.share(slot_ref, src_ref.at[pl.ds(c * size, size)], sends, recvs)
    for c in range(chunks):
        copies += group.pass_on(*wiring(c))
    for c in range(chunks):
        slot_ref, _, recvs = wiring(c)
        group.finish(slot_ref, recvs)
    own.wait()
    for copy in copies:
        copy.wait_send()


def gathered(block, owners, chunks):
    vmem = pl.BlockSpec(memory_space=pltpu.VMEM)
    return pl.pallas_call(
        functools.partial(gather_kernel, owners, chunks),
        name="context_gather",
        out_shape=jax.ShapeDtypeStruct((owners,) + block.shape, block.dtype),
        in_specs=[vmem],
        out_specs=vmem,
        scratch_shapes=[
            pltpu.SemaphoreType.DMA((owners, chunks)),
            pltpu.SemaphoreType.DMA((owners, chunks)),
            pltpu.SemaphoreType.DMA,
        ],
        compiler_params=pltpu.CompilerParams(
            collective_id=2, has_side_effects=True, vmem_limit_bytes=24 * 1024 * 1024
        ),
    )(block)


def cross_kernel(
    devices, parts, spans, off_ref, ctx_ref, outw_ref, nbr_ref, weight_ref, q_ref, next_ref,
    self_ref, out_ref, enc_ref, kv, result, earlier, handed, landed, send_sem, recv_sem,
    enc_send, enc_recv,
):
    me = lax.axis_index("seq")
    heads = q_ref.shape[1] // HD
    depth = enc_ref.shape[2]
    share = ctx_ref.shape[2]
    greet_next = lax.rem(me + 1, devices)
    group = Group(parts)
    greet(
        [{"seq": greet_next}, {"seq": lax.rem(me + devices - 1, devices)}]
        + [{"nb": peer} for peer in group.targets()]
    )
    order = [spans - 1] + list(range(spans - 1))
    enc_copies = []

    def wiring(c):
        rows = pl.ds(c * SET, SET)
        return (
            lambda slot: enc_ref.at[slot, rows],
            lambda t: enc_send.at[t, c],
            lambda slot: enc_recv.at[slot, c],
        )

    for c in order:
        rows = slice(c * SET, (c + 1) * SET)
        total = nbr_ref[rows, :].astype(jnp.float32)
        update = jnp.dot(
            ctx_ref[0, rows, :], outw_ref[0:share, :], preferred_element_type=jnp.float32
        )
        for n in range(1, parts):
            update += jnp.dot(
                ctx_ref[n, rows, :], outw_ref[n * share : (n + 1) * share, :],
                preferred_element_type=jnp.float32,
            )
        enc_ref[group.me, rows, :] = (total + update).astype(jnp.bfloat16)
        slot_ref, sends, recvs = wiring(c)
        enc_copies += group.share(slot_ref, slot_ref(group.me), sends, recvs)
    copy = pltpu.make_async_remote_copy(
        src_ref=handed, dst_ref=landed, send_sem=send_sem, recv_sem=recv_sem,
        device_id={"seq": greet_next}, device_id_type=MESH,
    )
    for c in order:
        rows = slice(c * SET, (c + 1) * SET)
        slot_ref, sends, recvs = wiring(c)
        enc_copies += group.pass_on(slot_ref, sends, recvs)
        group.finish(slot_ref, recvs)
        total = jnp.dot(
            enc_ref[0, rows, :], weight_ref[0:depth, :], preferred_element_type=jnp.float32
        )
        for n in range(1, parts):
            total += jnp.dot(
                enc_ref[n, rows, :], weight_ref[n * depth : (n + 1) * depth, :],
                preferred_element_type=jnp.float32,
            )
        kv[...] = total.astype(jnp.bfloat16)
        own_rows = slice(c * SPAN, (c + 1) * SPAN)
        for h in range(heads):
            lanes = slice(h * HD, (h + 1) * HD)
            if c == spans - 1:
                after = next_ref[:, lanes]
            else:
                after = q_ref[(c + 1) * SPAN : (c + 2) * SPAN, lanes]
            query = jnp.concatenate([q_ref[own_rows, lanes], after], axis=0)
            scores = lax.dot_general(
                query, kv[:, lanes], DOT_T, preferred_element_type=jnp.float32
            ) * (HD ** (-0.5))
            top = jnp.max(scores, axis=1, keepdims=True)
            weights = jnp.exp(scores - top)
            norm = jnp.sum(weights, axis=1, keepdims=True)
            summed = jnp.dot(
                weights.astype(jnp.bfloat16),
                kv[:, heads * HD + h * HD : heads * HD + (h + 1) * HD],
                preferred_element_type=jnp.float32,
            ) / norm
            result[own_rows, lanes] = summed[:SPAN]
            if c == spans - 1:
                handed[:, lanes] = summed[SPAN:]
            else:
                earlier[(c + 1) * SPAN : (c + 2) * SPAN, lanes] = summed[SPAN:]
        if c == spans - 1:
            copy.start()
    place = lax.broadcasted_iota(jnp.int32, (SPAN, q_ref.shape[1]), 0)
    for c in list(range(1, spans)) + [0]:
        rows = slice(c * SPAN, (c + 1) * SPAN)
        if c == 0:
            copy.wait()
            prior = jnp.where(me == 0, 0.0, landed[...])
        else:
            prior = earlier[rows, :]
        cross = jnp.where(place >= off_ref[c], result[rows, :], prior)
        out_ref[rows, :] = (self_ref[rows, :].astype(jnp.float32) + cross).astype(out_ref.dtype)
    for copy in enc_copies:
        copy.wait_send()


def cross_attention(offsets, ctx, output_part, nbr_part, weight, q, after, self_out, devices):
    parts = ctx.shape[0]
    rows, depth = nbr_part.shape
    tokens, head_cols = q.shape
    spans = offsets.shape[0]
    vmem = pl.BlockSpec(memory_space=pltpu.VMEM)
    return pl.pallas_call(
        functools.partial(cross_kernel, devices, parts, spans),
        name="cross_attention",
        out_shape=jax.ShapeDtypeStruct((tokens, head_cols), jnp.bfloat16),
        in_specs=[pl.BlockSpec(memory_space=pltpu.SMEM)] + [vmem] * 7,
        out_specs=vmem,
        scratch_shapes=[
            pltpu.VMEM((parts, rows, depth), jnp.bfloat16),
            pltpu.VMEM((SET, weight.shape[1]), jnp.bfloat16),
            pltpu.VMEM((tokens, head_cols), jnp.float32),
            pltpu.VMEM((tokens, head_cols), jnp.float32),
            pltpu.VMEM((SPAN, head_cols), jnp.float32),
            pltpu.VMEM((SPAN, head_cols), jnp.float32),
            pltpu.SemaphoreType.DMA,
            pltpu.SemaphoreType.DMA,
            pltpu.SemaphoreType.DMA((parts, spans)),
            pltpu.SemaphoreType.DMA((parts, spans)),
        ],
        compiler_params=pltpu.CompilerParams(
            collective_id=1, has_side_effects=True, vmem_limit_bytes=LIMIT
        ),
        cost_estimate=pl.CostEstimate(
            flops=2 * rows * parts * depth * weight.shape[1],
            bytes_accessed=20 * 1000 * 1000,
            transcendentals=0,
        ),
    )(offsets, ctx, output_part, nbr_part, weight, q, after, self_out)


def own_share(array, axis):
    share = array.shape[axis] // lax.axis_size("nb")
    return lax.dynamic_slice_in_dim(array, lax.axis_index("nb") * share, share, axis)


def local(
    q_self, k_self, v_self, q_cca, memory, database, nbr_block, span_offset,
    enc_query, enc_out, enc_gain, cca_kv,
):
    devices = lax.axis_size("seq")
    owners = lax.axis_size("nb")
    head_cols = q_self.shape[1]
    ids = lax.all_gather(nbr_block, "nb", axis=0, tiled=True)
    query_part = lax.all_gather(own_share(enc_query, 1), "seq", axis=0, tiled=True)
    output_part = lax.all_gather(own_share(enc_out, 1), "seq", axis=0, tiled=True)
    after = lax.ppermute(q_cca[:SPAN], "seq", [(i + 1, i) for i in range(devices - 1)])
    if (head_cols // HD) % devices == 0:
        self_out, db = exchanged_attention(q_self, k_self, v_self, database, devices, owners)
        db = db.reshape(-1, database.shape[1])
    else:
        db = lax.all_gather(database, "nb", axis=0, tiled=True)
        self_out = gathered_attention(q_self, k_self, v_self)
    ctx, nbr_part = encoder_context(
        ids, span_offset, db, enc_gain[None, :], query_part,
        own_share(memory[:, 0], 1), own_share(memory[:, 1], 1), output_part.shape[1],
    )
    ctx_full = gathered(ctx, owners, span_offset.shape[0])
    weight = cca_kv.reshape(cca_kv.shape[0], 2 * head_cols)
    return cross_attention(
        span_offset, ctx_full, output_part, nbr_part, weight, q_cca, after, self_out, devices
    )


def solution(mesh):
    in_specs = (
        P("seq", "nb"),
        P("seq", "nb"),
        P("seq", "nb"),
        P("seq", "nb"),
        P("seq", None, None),
        P(("seq", "nb"), None),
        P(("seq", "nb")),
        P("seq"),
        P("seq", None),
        P("seq", None),
        P(),
        P(None, None, "nb"),
    )
    out_specs = P("seq", "nb")
    return jax.shard_map(local, mesh=mesh, in_specs=in_specs, out_specs=out_specs, check_vma=False)
```
